32 devices in a mesh: gene: 4 (over y, core), rows: 8 (over z, x).
Axes of the slice: x: 2, y: 2, z: 4, core: 2. Of those that a mesh axis runs over, the one named last changes fastest.
Arguments:
- density: float32 [128, 256, 1024], P('gene', 'rows'), may hold values from 0.05 to 1, as said below
- effect_first: float32 [7], replicated, may hold values from 0.02 to 0.04
- effect_second: float32 [7], replicated, may hold values from 0 to 0.025
- decay_pair: float32 [2], replicated, may hold values from 0.08 to 0.5, as said below
- switch_rates: float32 [2, 7], replicated, may hold values from 0.1 to 3
- gene_place: int32 [7], replicated, may hold values from 0 to 6, each once
- bound_first: int32 [128], P('gene'), may hold values from 128 to 256
- bound_second: int32 [128], P('gene'), may hold values from 512 to 1024
Outputs:
- evolved: float32 [128, 256, 1024], P('gene', 'rows')
The draws below stay inside these ranges and needn't reach their ends.
Inputs may be any that keep to these rules, and one draw needn't show every extreme that they name: `gene_place`: a permutation: each bit 0 to 6 holds exactly one gene. `density`: positive probabilities. decay_pair[0] lies in 0.42 to 0.5 and decay_pair[1] in 0.08 to 0.22.
All inputs are finite; a program needn't handle non-finite values.
Results may differ from the reference program's by a relative error of at most 0.0003.
Values sent between devices are 32-bit elements; how exact they have to be, the bound alone decides.
A program may use at most 128 MiB of HBM per device.

```python
import math
import jax
import jax.numpy as jnp
from jax import lax

STATES = 128
GENES = 7
NB = 1024
ROWS_DEV = 32
SUB = 4
NA = 256


def draw_density(key, part):
    row_local = jnp.arange(NA) % ROWS_DEV
    edge_band = ((row_local <= SUB - 2) | (row_local >= ROWS_DEV - SUB + 1)).astype(jnp.float32)[None, :, None]
    uniform_part = jax.random.uniform(key, (STATES, NA, NB), jnp.float32)
    base_value = jnp.exp(jnp.log(0.3) * uniform_part)
    factor = 1.0 - 0.8 * edge_band
    return (base_value * factor).astype(jnp.float32)


def draw_decay_pair(key, part):
    uniform_part = jax.random.uniform(key, (2,), jnp.float32)
    first_decay = 0.42 + 0.08 * uniform_part[0]
    second_decay = 0.08 + 0.14 * uniform_part[1]
    return jnp.stack([first_decay, second_decay]).astype(jnp.float32)


def place_ends(array, stream_key, low, high):
    index_at = [jax.random.randint(jax.random.fold_in(stream_key, axis), (), 0, length) for axis, length in enumerate(array.shape)]
    longest = array.shape.index(max(array.shape))
    neighbour = index_at[:longest] + [(index_at[longest] + 1) % array.shape[longest]] + index_at[longest + 1:]
    return array.at[tuple(index_at)].set(low).at[tuple(neighbour)].set(high)


def setup_inputs(seed: int = 0) -> dict:
    keys = jax.random.split(jax.random.key(seed), 9)
    return {
        "density": draw_density(jax.random.fold_in(keys[8], 71), 0),
        "effect_first": jnp.clip(jax.random.uniform(keys[1], (GENES,), jnp.float32, 0.02, 0.04), 0.02, 0.04),
        "effect_second": jnp.clip(jax.random.uniform(keys[2], (GENES,), jnp.float32, 0.0, 0.025), 0.0, 0.025),
        "decay_pair": draw_decay_pair(jax.random.fold_in(keys[8], 71), 0),
        "switch_rates": jnp.clip(jnp.exp(jax.random.uniform(keys[4], (2, GENES), jnp.float32, math.log(0.1), math.log(3.0))), 0.1, 3.0),
        "gene_place": jax.random.permutation(keys[5], GENES).astype(jnp.int32),
        "bound_first": place_ends(jax.random.randint(keys[6], (STATES,), NA // 2, NA + 1), jax.random.fold_in(keys[6], 1), NA // 2, NA).astype(jnp.int32),
        "bound_second": place_ends(jax.random.randint(keys[7], (STATES,), NB // 2, NB + 1), jax.random.fold_in(keys[7], 1), NB // 2, NB).astype(jnp.int32),
    }


def state_rates(states, gene_place, effect_first, effect_second):
    bits = ((states[:, None] >> gene_place[None, :]) & 1).astype(jnp.float32)
    birth_one = 0.02 + jnp.sum(bits * effect_first[None, :], axis=1)
    birth_two = 0.02 + jnp.sum(bits * effect_second[None, :], axis=1)
    return birth_one, birth_two


def stencil_step(padded, first_row, birth_one, birth_two, decay_pair, limit_one, limit_two, total_rows):
    count = padded.shape[1]
    width = padded.shape[2]
    rows_index = (first_row - 1 + jnp.arange(count)).astype(jnp.float32)[None, :, None]
    cols_index = jnp.arange(width).astype(jnp.float32)[None, None, :]
    grow_rows = birth_one * width / (width + 3.0 * cols_index) * (rows_index + 1.0 < limit_one).astype(jnp.float32)
    grow_cols = birth_two * (total_rows + 3.0 * rows_index) / (4.0 * total_rows) * (cols_index + 1.0 < limit_two).astype(jnp.float32)
    fall_rows = decay_pair[0] * rows_index / total_rows
    fall_cols = decay_pair[1] * cols_index / width
    centre = padded[:, 1:-1]
    leave = (grow_rows + grow_cols + fall_rows + fall_cols)[:, 1:-1]
    up_flow = grow_rows * padded
    down_flow = fall_rows * padded
    side_grow = grow_cols[:, 1:-1] * centre
    side_fall = fall_cols * centre
    zero_col = jnp.zeros_like(centre[..., :1])
    result = centre * (1.0 - leave) + up_flow[:, :-2] + down_flow[:, 2:]
    result = result + jnp.concatenate([zero_col, side_grow[..., :-1]], axis=2)
    return result + jnp.concatenate([side_fall[..., 1:], zero_col], axis=2)


def switch_factors(gene_place, switch_rates):
    match = (gene_place[None, :] == jnp.arange(GENES)[:, None]).astype(jnp.float32)
    rate_on = jnp.sum(match * switch_rates[0][None, :], axis=1)
    rate_off = jnp.sum(match * switch_rates[1][None, :], axis=1)
    total = rate_on + rate_off
    fading = jnp.exp(-total)
    return ((rate_off + rate_on * fading) / total, rate_off * (1.0 - fading) / total,
            rate_on * (1.0 - fading) / total, (rate_on + rate_off * fading) / total)


def switch_one(block, bit, factors):
    shape = block.shape
    view = block.reshape((shape[0] // (2 << bit), 2, 1 << bit) + shape[1:])
    low = view[:, 0]
    high = view[:, 1]
    new_low = factors[0][bit] * low + factors[1][bit] * high
    new_high = factors[2][bit] * low + factors[3][bit] * high
    return jnp.stack([new_low, new_high], axis=1).reshape(shape)


def half_step(density, birth_one, birth_two, decay_pair, bound_first, bound_second):
    def evolve(item):
        block, first_rate, second_rate, first_limit, second_limit = item
        current = block[None]
        for step in range(SUB):
            padded = jnp.pad(current, ((0, 0), (1, 1), (0, 0)))
            current = stencil_step(padded, 0, first_rate.reshape(1, 1, 1), second_rate.reshape(1, 1, 1), decay_pair,
                                   first_limit.astype(jnp.float32).reshape(1, 1, 1),
                                   second_limit.astype(jnp.float32).reshape(1, 1, 1), jnp.float32(NA))
        return current[0]

    return lax.map(evolve, (density, birth_one, birth_two, bound_first, bound_second))


def reference(density, effect_first, effect_second, decay_pair, switch_rates, gene_place, bound_first, bound_second):
    states = jnp.arange(STATES).astype(jnp.int32)
    birth_one, birth_two = state_rates(states, gene_place, effect_first, effect_second)
    first = half_step(density, birth_one, birth_two, decay_pair, bound_first, bound_second)
    factors = switch_factors(gene_place, switch_rates)
    switched = first
    for bit in range(GENES):
        switched = switch_one(switched, bit, factors)
    return half_step(switched, birth_one, birth_two, decay_pair, bound_first, bound_second)
```

```python
import functools

import jax
import jax.numpy as jnp
from jax import lax
from jax.experimental import pallas as pl
from jax.experimental.pallas import tpu as pltpu
from jax.sharding import PartitionSpec as P

GENES = 7
SUB = 4
TILE = 8
LANES = 128
EARLY = 10
MESH = pl.DeviceIdType.MESH


def state_rates(states, gene_place, effect_first, effect_second):
    bits = (states[:, None] >> gene_place[None, :] & 1).astype(jnp.float32)
    birth_one = 0.02 + jnp.sum(bits * effect_first[None, :], axis=1)
    birth_two = 0.02 + jnp.sum(bits * effect_second[None, :], axis=1)
    return (birth_one, birth_two)


def switch_factors(gene_place, switch_rates):
    match = (gene_place[None, :] == jnp.arange(GENES)[:, None]).astype(jnp.float32)
    rate_on = jnp.sum(match * switch_rates[0][None, :], axis=1)
    rate_off = jnp.sum(match * switch_rates[1][None, :], axis=1)
    total = rate_on + rate_off
    fading = jnp.exp(-total)
    return jnp.concatenate([
        (rate_off + rate_on * fading) / total,
        rate_off * (1.0 - fading) / total,
        rate_on * (1.0 - fading) / total,
        (rate_on + rate_off * fading) / total,
    ])


def kernel(
    count, rows, width, peers, total_rows,
    x_ref, birth_ref, bound_ref, grow_ref, curve_ref, fall_ref, decay_ref, factor_ref,
    out_ref,
    main, edge, late, late_edge, *rest,
):
    stages = len(rest) - 6
    arrived = rest[:stages]
    send_sem, recv_sem, halo_send, halo_recv, late_send, late_recv = rest[stages:]
    tiles = count // TILE
    local_bits = count.bit_length() - 1
    gene = lax.axis_index("gene")
    place = lax.axis_index("rows")
    first = place * rows
    partners = [gene + (1 << q) - 2 * (gene & (1 << q)) for q in range(stages)]
    has_prev, has_next = place > 0, place < peers - 1

    barrier = pltpu.get_barrier_semaphore()
    for partner in partners:
        pl.semaphore_signal(barrier, inc=1, device_id=(partner, place), device_id_type=MESH)

    @pl.when(has_prev)
    def _():
        pl.semaphore_signal(barrier, inc=1, device_id=(gene, place - 1), device_id_type=MESH)

    @pl.when(has_next)
    def _():
        pl.semaphore_signal(barrier, inc=1, device_id=(gene, place + 1), device_id_type=MESH)

    def loop(low, high, step):
        def run(i, carry):
            step(i)
            return carry
        lax.fori_loop(low, high, run, 0)

    def part(i):
        return pl.ds(TILE * i, TILE)

    def wide(value):
        return jnp.concatenate([value] * (width // LANES), axis=1)

    def load(row):
        return x_ref[:, row, :]

    def update(buf, slot, row, out=False):
        level = (first + row).astype(jnp.float32)
        side = (total_rows + 3.0 * level) * (1.0 / (4.0 * total_rows))
        drop = decay_ref[0] * level * (1.0 / total_rows)
        drop_next = decay_ref[0] * (level + 1.0) * (1.0 / total_rows)
        stay = 1.0 - drop
        for i in range(tiles):
            above = buf[slot, part(i), :]
            here = buf[slot + 1, part(i), :]
            below = buf[slot + 2, part(i), :]
            birth, bound = birth_ref[part(i), :], bound_ref[part(i), :]
            rise = wide(jnp.where(level + 1.0 < bound, birth, 0.0))
            rise_above = wide(jnp.where(level < bound, birth, 0.0))
            right = here * (grow_ref[part(i), :] * side)
            left = here * fall_ref[...]
            value = here * stay + drop_next * below
            value = value + curve_ref[...] * (rise_above * above - rise * here)
            value = value + (pltpu.roll(right, 1, 1) - right)
            value = value + (pltpu.roll(left, width - 1, 1) - left)
            if out:
                out_ref[part(i), row, :] = value
            else:
                buf[slot, part(i), :] = value

    def triangle(buf, slots, base, last):
        for t in range(1, last + 1):
            loop(0, slots - 2 * t, lambda j, t=t: update(buf, j, base + j + t))

    def wave(buf, k, out=False):
        for t in range(1, SUB + 1):
            slot = k - 2 * (t - 1)
            update(buf, slot, slot + t, out=out and t == SUB)

    def slot_of(row):
        return lax.rem(row + rows - SUB, rows)

    def mine(q, row):
        return main.at[slot_of(row)] if q == 0 else arrived[q - 1].at[row]

    def exchange(q, row):
        return pltpu.make_async_remote_copy(
            src_ref=mine(q, row), dst_ref=arrived[q].at[row],
            send_sem=send_sem.at[q, row], recv_sem=recv_sem.at[q, row],
            device_id=(partners[q], place), device_id_type=MESH)

    def factor(kind, bit):
        return factor_ref[kind * GENES + bit]

    def mix(q, row):
        bit = local_bits + q
        on = (gene >> q) & 1 == 1
        keep = jnp.where(on, factor(3, bit), factor(0, bit))
        take = jnp.where(on, factor(2, bit), factor(1, bit))
        own = mine(q, row)
        return [keep * own[part(i), :] + take * arrived[q][row, part(i), :] for i in range(tiles)]

    def advance(q, row):
        exchange(q, row).wait_recv()
        for i, value in enumerate(mix(q, row)):
            arrived[q][row, part(i), :] = value
        exchange(q + 1, row).start()

    def finish(row):
        q = stages - 1
        exchange(q, row).wait_recv()
        blocks = mix(q, row)
        index = lax.broadcasted_iota(jnp.int32, (TILE, LANES), 0)
        for bit in range(3):
            on = (index >> bit) & 1 == 1
            keep = wide(jnp.where(on, factor(3, bit), factor(0, bit)))
            take = wide(jnp.where(on, factor(2, bit), factor(1, bit)))
            swap = wide(on)
            gap = 1 << bit
            mixed = []
            for block in blocks:
                other = pltpu.roll(block, gap, 0)
                if 2 * gap != TILE:
                    other = jnp.where(swap, other, pltpu.roll(block, TILE - gap, 0))
                mixed.append(keep * block + take * other)
            blocks = mixed
        for bit in range(3, local_bits):
            gap = 1 << (bit - 3)
            mixed = list(blocks)
            for i in range(tiles):
                if not i & gap:
                    low, high = blocks[i], blocks[i + gap]
                    mixed[i] = factor(0, bit) * low + factor(1, bit) * high
                    mixed[i + gap] = factor(2, bit) * low + factor(3, bit) * high
            blocks = mixed
        for i in range(tiles):
            late[row, part(i), :] = blocks[i]

    def halo(grid, rim, sends, recvs):
        upward = pltpu.make_async_remote_copy(
            src_ref=grid.at[pl.ds(rows - SUB, SUB)], dst_ref=rim.at[pl.ds(0, SUB)],
            send_sem=sends.at[0], recv_sem=recvs.at[0],
            device_id=(gene, place + 1), device_id_type=MESH)
        downward = pltpu.make_async_remote_copy(
            src_ref=rim.at[pl.ds(SUB, SUB)], dst_ref=grid.at[pl.ds(rows, SUB)],
            send_sem=sends.at[1], recv_sem=recvs.at[1],
            device_id=(gene, place - 1), device_id_type=MESH)
        return upward, downward

    def halo_start(copies):
        @pl.when(has_next)
        def _():
            copies[0].start()

        @pl.when(has_prev)
        def _():
            copies[1].start()

    def halo_top(copies, rim):
        @pl.when(has_prev)
        def _():
            copies[1].wait_send()
            copies[0].wait_recv()

        @pl.when(jnp.logical_not(has_prev))
        def _():
            rim[pl.ds(0, SUB)] = jnp.zeros((SUB, count, width), jnp.float32)

    def halo_bottom(copies, grid):
        @pl.when(has_next)
        def _():
            copies[0].wait_send()
            copies[1].wait_recv()

        @pl.when(jnp.logical_not(has_next))
        def _():
            grid[pl.ds(rows, SUB)] = jnp.zeros((SUB, count, width), jnp.float32)

    def load_both(row):
        value = load(row)
        main[row] = value
        edge[SUB + row] = value

    def load_main(row):
        main[row] = load(row)

    loop(0, SUB, load_both)
    loop(rows - SUB, rows, load_main)
    met = stages + jnp.where(has_prev, 1, 0) + jnp.where(has_next, 1, 0)
    pl.semaphore_wait(barrier, met)

    early_halo = halo(main, edge, halo_send, halo_recv)
    halo_start(early_halo)
    loop(SUB, 2 * SUB, load_both)
    triangle(main, 2 * SUB, 0, SUB - 1)

    def produce(k):
        @pl.when(k + 2 < rows - SUB)
        def _():
            load_main(k + 2)
        wave(main, k)
        exchange(0, k - 2).start()

    def produce_and_pass(k):
        produce(k)
        advance(0, k - 3)

    early = SUB + EARLY
    produce(6)
    loop(7, early + 3, produce_and_pass)
    loop(early + 3, rows - SUB, produce)
    halo_bottom(early_halo, main)
    loop(rows - SUB, rows + 2, produce)
    halo_top(early_halo, edge)
    triangle(edge, 3 * SUB, -SUB, SUB)

    def give(row):
        main[rows - SUB + row] = edge[row]
        exchange(0, row).start()

    loop(0, SUB, give)
    order = [(SUB, early), (rows - SUB, rows), (0, SUB), (early, rows - SUB)]
    for low, high in order[1:]:
        loop(low, high, lambda row: advance(0, row))
    for q in range(1, stages - 1):
        for low, high in order:
            loop(low, high, lambda row, q=q: advance(q, row))

    for low, high in order[:-1]:
        loop(low, high, finish)

    def copy_edge(row):
        late_edge[SUB + row] = late[row]

    loop(0, 2 * SUB, copy_edge)
    late_halo = halo(late, late_edge, late_send, late_recv)
    halo_start(late_halo)

    def emit(k):
        wave(late, k, out=True)

    def finish_and_emit(k):
        finish(k + 2)
        emit(k)

    triangle(late, 2 * SUB, 0, SUB - 1)
    loop(6, early - 2, emit)
    loop(early - 2, rows - SUB - 6, finish_and_emit)
    halo_top(late_halo, late_edge)
    triangle(late_edge, 3 * SUB, -SUB, SUB - 1)
    loop(0, SUB, lambda j: update(late_edge, j, j, out=True))
    loop(rows - SUB - 6, rows - SUB - 2, finish_and_emit)
    halo_bottom(late_halo, late)
    loop(rows - SUB - 2, rows + 2, emit)
    for q in range(stages):
        loop(0, rows, lambda row, q=q: exchange(q, row).wait_send())


def body(
    peers,
    genes,
    density,
    effect_first,
    effect_second,
    decay_pair,
    switch_rates,
    gene_place,
    bound_first,
    bound_second,
):
    count, rows, width = density.shape
    stages = genes.bit_length() - 1
    states = lax.axis_index("gene") * count + jnp.arange(count)
    birth_one, birth_two = state_rates(states, gene_place, effect_first, effect_second)
    cols = jnp.arange(width).astype(jnp.float32)
    birth = jnp.broadcast_to(birth_one[:, None], (count, LANES))
    bound = jnp.broadcast_to(bound_first.astype(jnp.float32)[:, None], (count, LANES))
    grow = jnp.where(
        cols[None, :] + 1.0 < bound_second.astype(jnp.float32)[:, None], birth_two[:, None], 0.0)
    curve = jnp.broadcast_to(width / (width + 3.0 * cols), (TILE, width))
    fall = jnp.broadcast_to(decay_pair[1] * cols / width, (TILE, width))
    factors = switch_factors(gene_place, switch_rates)
    row = (count, width)
    vmem = pl.BlockSpec(memory_space=pltpu.VMEM)
    smem = pl.BlockSpec(memory_space=pltpu.SMEM)
    return pl.pallas_call(
        functools.partial(kernel, count, rows, width, peers, float(rows * peers)),
        out_shape=jax.ShapeDtypeStruct(density.shape, jnp.float32),
        in_specs=[vmem] * 6 + [smem] * 2,
        out_specs=vmem,
        scratch_shapes=[
            pltpu.VMEM((rows + SUB,) + row, jnp.float32),
            pltpu.VMEM((3 * SUB,) + row, jnp.float32),
            pltpu.VMEM((rows + SUB,) + row, jnp.float32),
            pltpu.VMEM((3 * SUB,) + row, jnp.float32),
        ] + [pltpu.VMEM((rows,) + row, jnp.float32)] * stages + [
            pltpu.SemaphoreType.DMA((stages, rows)),
            pltpu.SemaphoreType.DMA((stages, rows)),
            pltpu.SemaphoreType.DMA((2,)),
            pltpu.SemaphoreType.DMA((2,)),
            pltpu.SemaphoreType.DMA((2,)),
            pltpu.SemaphoreType.DMA((2,)),
        ],
        compiler_params=pltpu.CompilerParams(
            collective_id=0, has_side_effects=True, vmem_limit_bytes=48 * 1024 * 1024),
    )(density, birth, bound, grow, curve, fall, decay_pair, factors)


def solution(mesh):
    placed = (P("gene", "rows", None), P(), P(), P(), P(), P(), P("gene"), P("gene"))
    return jax.shard_map(
        functools.partial(body, mesh.shape["rows"], mesh.shape["gene"]),
        mesh=mesh, in_specs=placed, out_specs=P("gene", "rows", None), check_vma=False,
    )
```

```python
import functools

import jax
import jax.numpy as jnp
from jax import lax
from jax.experimental import pallas as pl
from jax.experimental.pallas import tpu as pltpu
from jax.sharding import PartitionSpec as P

GENES = 7
SUB = 4
TILE = 8
LANES = 128
EARLY = 10
MESH = pl.DeviceIdType.MESH


def kernel(
    count, rows, width, peers, total_rows,
    density_ref, effect_one, effect_two, decay_ref, rates_ref, place_ref, bound_one, bound_two,
    result_ref,
    x_ref, out_ref, birth_ref, bound_ref, limit_ref, grow_ref, curve_ref, fall_ref, factor_ref,
    main, edge, late, late_edge, *rest,
):
    stages = len(rest) - 8
    arrived = rest[:stages]
    (send_sem, recv_sem, halo_send, halo_recv, late_send, late_recv, in_sem,
     out_sem) = rest[stages:]
    tiles = count // TILE
    local_bits = count.bit_length() - 1
    gene = lax.axis_index("gene")
    place = lax.axis_index("rows")
    first = place * rows
    partners = [gene + (1 << q) - 2 * (gene & (1 << q)) for q in range(stages)]
    has_prev, has_next = place > 0, place < peers - 1

    barrier = pltpu.get_barrier_semaphore()
    for partner in partners:
        pl.semaphore_signal(barrier, inc=1, device_id=(partner, place), device_id_type=MESH)

    @pl.when(has_prev)
    def _():
        pl.semaphore_signal(barrier, inc=1, device_id=(gene, place - 1), device_id_type=MESH)

    @pl.when(has_next)
    def _():
        pl.semaphore_signal(barrier, inc=1, device_id=(gene, place + 1), device_id_type=MESH)

    def fetch(block):
        piece = pl.ds(TILE * block, TILE)
        return pltpu.make_async_copy(
            density_ref.at[:, piece, :], x_ref.at[:, piece, :], in_sem.at[block])

    def deliver(block):
        piece = pl.ds(TILE * block, TILE)
        return pltpu.make_async_copy(
            out_ref.at[:, piece, :], result_ref.at[:, piece, :], out_sem.at[block])

    blocks_in = rows // TILE
    fetch_order = [0, blocks_in - 1] + list(range(1, blocks_in - 1))
    for block in fetch_order:
        fetch(block).start()

    def loop(low, high, step):
        def run(i, carry):
            step(i)
            return carry
        lax.fori_loop(low, high, run, 0)

    def part(i):
        return pl.ds(TILE * i, TILE)

    def wide(value):
        return jnp.concatenate([value] * (width // LANES), axis=1)

    def by_bit(values, bit):
        total = jnp.float32(0.0)
        for g in range(GENES):
            total = total + jnp.where(place_ref[g] == bit, values(g), 0.0)
        return total

    def spread(s):
        line = pl.ds(s, 1)
        bound_ref[line, :] = jnp.full((1, LANES), bound_one[s].astype(jnp.float32))
        limit_ref[line, :] = jnp.full((1, LANES), bound_two[s].astype(jnp.float32))

    def prepare():
        loop(0, count, spread)
        cols = lax.broadcasted_iota(jnp.int32, (TILE, width), 1).astype(jnp.float32)
        curve_ref[...] = width / (width + 3.0 * cols)
        fall_ref[...] = decay_ref[1] * cols * (1.0 / width)
        first_effects = [by_bit(lambda g: effect_one[g], bit) for bit in range(GENES)]
        second_effects = [by_bit(lambda g: effect_two[g], bit) for bit in range(GENES)]
        line = lax.broadcasted_iota(jnp.int32, (TILE, LANES), 0)
        for i in range(tiles):
            state = gene * count + TILE * i + line
            one = jnp.full((TILE, LANES), 0.02, jnp.float32)
            two = jnp.full((TILE, LANES), 0.02, jnp.float32)
            for bit in range(GENES):
                held = ((state >> bit) & 1).astype(jnp.float32)
                one = one + held * first_effects[bit]
                two = two + held * second_effects[bit]
            birth_ref[part(i), :] = one
            grow_ref[part(i), :] = jnp.where(
                cols + 1.0 < wide(limit_ref[part(i), :]), wide(two), 0.0)
        for bit in range(GENES):
            rate_on = jnp.full((TILE, LANES), by_bit(lambda g: rates_ref[0, g], bit))
            rate_off = jnp.full((TILE, LANES), by_bit(lambda g: rates_ref[1, g], bit))
            total = rate_on + rate_off
            fading = jnp.exp(-total)
            factor_ref[bit] = (rate_off + rate_on * fading) / total
            factor_ref[GENES + bit] = rate_off * (1.0 - fading) / total
            factor_ref[2 * GENES + bit] = rate_on * (1.0 - fading) / total
            factor_ref[3 * GENES + bit] = (rate_on + rate_off * fading) / total

    def load(row):
        return x_ref[:, row, :]

    def update(buf, slot, row, out=False):
        level = (first + row).astype(jnp.float32)
        side = (total_rows + 3.0 * level) * (1.0 / (4.0 * total_rows))
        drop = decay_ref[0] * level * (1.0 / total_rows)
        drop_next = decay_ref[0] * (level + 1.0) * (1.0 / total_rows)
        fall, curve = fall_ref[...], curve_ref[...]
        stay = (1.0 - drop) - fall
        values = []
        for i in range(tiles):
            above = buf[slot, part(i), :]
            here = buf[slot + 1, part(i), :]
            below = buf[slot + 2, part(i), :]
            birth, bound = birth_ref[part(i), :], bound_ref[part(i), :]
            rise = wide(jnp.where(level + 1.0 < bound, birth, 0.0))
            rise_above = wide(jnp.where(level < bound, birth, 0.0))
            right = here * (grow_ref[part(i), :] * side)
            left = here * fall
            value = here * stay + drop_next * below
            value = value + curve * (rise_above * above - rise * here)
            value = value + (pltpu.roll(right, 1, 1) - right)
            values.append(value + pltpu.roll(left, width - 1, 1))
        for i, value in enumerate(values):
            if out:
                out_ref[part(i), row, :] = value
            else:
                buf[slot, part(i), :] = value

    def triangle(buf, slots, base, last):
        for t in range(1, last + 1):
            loop(0, slots - 2 * t, lambda j, t=t: update(buf, j, base + j + t))

    def wave(buf, k, out=False):
        for t in range(1, SUB + 1):
            slot = k - 2 * (t - 1)
            update(buf, slot, slot + t, out=out and t == SUB)

    def slot_of(row):
        return lax.rem(row + rows - SUB, rows)

    def mine(q, row):
        return main.at[slot_of(row)] if q == 0 else arrived[q - 1].at[row]

    def exchange(q, row):
        return pltpu.make_async_remote_copy(
            src_ref=mine(q, row), dst_ref=arrived[q].at[row],
            send_sem=send_sem.at[q, row], recv_sem=recv_sem.at[q, row],
            device_id=(partners[q], place), device_id_type=MESH)

    def factor(kind, bit):
        return factor_ref[kind * GENES + bit]

    def mix(q, row):
        bit = local_bits + q
        on = (gene >> q) & 1 == 1
        keep = wide(jnp.where(on, factor(3, bit), factor(0, bit)))
        take = wide(jnp.where(on, factor(2, bit), factor(1, bit)))
        own = mine(q, row)
        return [keep * own[part(i), :] + take * arrived[q][row, part(i), :] for i in range(tiles)]

    def advance(q, row):
        exchange(q, row).wait_recv()
        for i, value in enumerate(mix(q, row)):
            arrived[q][row, part(i), :] = value
        exchange(q + 1, row).start()

    def finish(row):
        q = stages - 1
        exchange(q, row).wait_recv()
        blocks = mix(q, row)
        index = lax.broadcasted_iota(jnp.int32, (TILE, LANES), 0)
        for bit in range(3):
            on = (index >> bit) & 1 == 1
            keep = wide(jnp.where(on, factor(3, bit), factor(0, bit)))
            take = wide(jnp.where(on, factor(2, bit), factor(1, bit)))
            swap = wide(on)
            gap = 1 << bit
            mixed = []
            for block in blocks:
                other = pltpu.roll(block, gap, 0)
                if 2 * gap != TILE:
                    other = jnp.where(swap, other, pltpu.roll(block, TILE - gap, 0))
                mixed.append(keep * block + take * other)
            blocks = mixed
        for bit in range(3, local_bits):
            gap = 1 << (bit - 3)
            mixed = list(blocks)
            for i in range(tiles):
                if not i & gap:
                    low, high = blocks[i], blocks[i + gap]
                    mixed[i] = wide(factor(0, bit)) * low + wide(factor(1, bit)) * high
                    mixed[i + gap] = wide(factor(2, bit)) * low + wide(factor(3, bit)) * high
            blocks = mixed
        for i in range(tiles):
            late[row, part(i), :] = blocks[i]

    def halo(grid, rim, sends, recvs):
        upward = pltpu.make_async_remote_copy(
            src_ref=grid.at[pl.ds(rows - SUB, SUB)], dst_ref=rim.at[pl.ds(0, SUB)],
            send_sem=sends.at[0], recv_sem=recvs.at[0],
            device_id=(gene, place + 1), device_id_type=MESH)
        downward = pltpu.make_async_remote_copy(
            src_ref=rim.at[pl.ds(SUB, SUB)], dst_ref=grid.at[pl.ds(rows, SUB)],
            send_sem=sends.at[1], recv_sem=recvs.at[1],
            device_id=(gene, place - 1), device_id_type=MESH)
        return upward, downward

    def halo_start(copies):
        @pl.when(has_next)
        def _():
            copies[0].start()

        @pl.when(has_prev)
        def _():
            copies[1].start()

    def halo_top(copies, rim):
        @pl.when(has_prev)
        def _():
            copies[1].wait_send()
            copies[0].wait_recv()

        @pl.when(jnp.logical_not(has_prev))
        def _():
            rim[pl.ds(0, SUB)] = jnp.zeros((SUB, count, width), jnp.float32)

    def halo_bottom(copies, grid):
        @pl.when(has_next)
        def _():
            copies[0].wait_send()
            copies[1].wait_recv()

        @pl.when(jnp.logical_not(has_next))
        def _():
            grid[pl.ds(rows, SUB)] = jnp.zeros((SUB, count, width), jnp.float32)

    def load_both(row):
        value = load(row)
        main[row] = value
        edge[SUB + row] = value

    def load_main(row):
        main[row] = load(row)

    prepare()
    for block in fetch_order[:2]:
        fetch(block).wait()
    loop(0, SUB, load_both)
    loop(rows - SUB, rows, load_main)
    met = stages + jnp.where(has_prev, 1, 0) + jnp.where(has_next, 1, 0)
    pl.semaphore_wait(barrier, met)

    early_halo = halo(main, edge, halo_send, halo_recv)
    halo_start(early_halo)
    loop(SUB, 2 * SUB, load_both)
    for block in fetch_order[2:]:
        fetch(block).wait()
    triangle(main, 2 * SUB, 0, SUB - 1)

    def produce(k):
        @pl.when(k + 2 < rows - SUB)
        def _():
            load_main(k + 2)
        wave(main, k)
        exchange(0, k - 2).start()

    def produce_and_pass(k):
        produce(k)
        advance(0, k - 3)

    early = SUB + EARLY
    produce(6)
    loop(7, early + 3, produce_and_pass)
    loop(early + 3, rows - SUB, produce)
    halo_bottom(early_halo, main)
    loop(rows - SUB, rows + 2, produce)
    halo_top(early_halo, edge)
    triangle(edge, 3 * SUB, -SUB, SUB)

    def give(row):
        main[rows - SUB + row] = edge[row]
        exchange(0, row).start()

    loop(0, SUB, give)
    order = [(SUB, early), (rows - SUB, rows), (0, SUB), (early, rows - SUB)]
    for low, high in order[1:]:
        loop(low, high, lambda row: advance(0, row))
    for q in range(1, stages - 1):
        for low, high in order:
            loop(low, high, lambda row, q=q: advance(q, row))

    for low, high in order[:-1]:
        loop(low, high, finish)

    def copy_edge(row):
        late_edge[SUB + row] = late[row]

    loop(0, 2 * SUB, copy_edge)
    late_halo = halo(late, late_edge, late_send, late_recv)
    halo_start(late_halo)

    def emit(k):
        wave(late, k, out=True)

    def finish_and_emit(k):
        finish(k + 2)
        emit(k)

    triangle(late, 2 * SUB, 0, SUB - 1)
    loop(6, early - 2, emit)
    loop(early - 2, rows - SUB - 6, finish_and_emit)
    deliver(1).start()
    halo_top(late_halo, late_edge)
    triangle(late_edge, 3 * SUB, -SUB, SUB - 1)
    loop(0, SUB, lambda j: update(late_edge, j, j, out=True))
    deliver(0).start()
    loop(rows - SUB - 6, rows - SUB - 2, finish_and_emit)
    deliver(2).start()
    halo_bottom(late_halo, late)
    loop(rows - SUB - 2, rows + 2, emit)
    deliver(3).start()
    for q in range(stages):
        loop(0, rows, lambda row, q=q: exchange(q, row).wait_send())
    for block in range(blocks_in):
        deliver(block).wait()


def body(peers, genes, density, *params):
    count, rows, width = density.shape
    stages = genes.bit_length() - 1
    row = (count, width)
    smem = pl.BlockSpec(memory_space=pltpu.SMEM)
    whole = pl.BlockSpec(memory_space=pl.ANY)

    def vmem(*shape):
        return pltpu.VMEM(shape, jnp.float32)

    return pl.pallas_call(
        functools.partial(kernel, count, rows, width, peers, float(rows * peers)),
        out_shape=jax.ShapeDtypeStruct(density.shape, jnp.float32),
        in_specs=[whole] + [smem] * len(params),
        out_specs=whole,
        scratch_shapes=[
            vmem(*density.shape),
            vmem(*density.shape),
            vmem(count, LANES),
            vmem(count, LANES),
            vmem(count, LANES),
            vmem(*row),
            vmem(TILE, width),
            vmem(TILE, width),
            vmem(4 * GENES, TILE, LANES),
            vmem(rows + SUB, *row),
            vmem(3 * SUB, *row),
            vmem(rows + SUB, *row),
            vmem(3 * SUB, *row),
        ] + [vmem(rows, *row)] * stages + [
            pltpu.SemaphoreType.DMA((stages, rows)),
            pltpu.SemaphoreType.DMA((stages, rows)),
            pltpu.SemaphoreType.DMA((2,)),
            pltpu.SemaphoreType.DMA((2,)),
            pltpu.SemaphoreType.DMA((2,)),
            pltpu.SemaphoreType.DMA((2,)),
            pltpu.SemaphoreType.DMA((rows // TILE,)),
            pltpu.SemaphoreType.DMA((rows // TILE,)),
        ],
        compiler_params=pltpu.CompilerParams(
            collective_id=0, has_side_effects=True, vmem_limit_bytes=60 * 1024 * 1024),
    )(density, *params)


def solution(mesh):
    placed = (P("gene", "rows", None), P(), P(), P(), P(), P(), P("gene"), P("gene"))
    return jax.shard_map(
        functools.partial(body, mesh.shape["rows"], mesh.shape["gene"]),
        mesh=mesh, in_specs=placed, out_specs=P("gene", "rows", None), check_vma=False,
    )
```

```python
import functools

import jax
import jax.numpy as jnp
import numpy as np
from jax import lax
from jax.experimental import pallas as pl
from jax.experimental.pallas import tpu as pltpu
from jax.sharding import PartitionSpec as P

GENES = 7
SUB = 4
TILE = 8
LANES = 128
EARLY = 10
MESH = pl.DeviceIdType.MESH


def kernel(
    count, rows, width, peers, total_rows,
    density_ref, param_ref, out_ref,
    x_ref, birth_ref, bound_ref, limit_ref, grow_ref, curve_ref, fall_ref, factor_ref,
    main, edge, late, late_edge, *rest,
):
    stages = len(rest) - 7
    arrived = rest[:stages]
    send_sem, recv_sem, halo_send, halo_recv, late_send, late_recv, in_sem = rest[stages:]
    tiles = count // TILE
    local_bits = count.bit_length() - 1
    gene = lax.axis_index("gene")
    place = lax.axis_index("rows")
    first = place * rows
    partners = [gene + (1 << q) - 2 * (gene & (1 << q)) for q in range(stages)]
    has_prev, has_next = place > 0, place < peers - 1

    barrier = pltpu.get_barrier_semaphore()
    for partner in partners:
        pl.semaphore_signal(barrier, inc=1, device_id=(partner, place), device_id_type=MESH)

    @pl.when(has_prev)
    def _():
        pl.semaphore_signal(barrier, inc=1, device_id=(gene, place - 1), device_id_type=MESH)

    @pl.when(has_next)
    def _():
        pl.semaphore_signal(barrier, inc=1, device_id=(gene, place + 1), device_id_type=MESH)

    def fetch(block):
        piece = pl.ds(TILE * block, TILE)
        return pltpu.make_async_copy(
            density_ref.at[:, piece, :], x_ref.at[:, piece, :], in_sem.at[block])

    fetch_order = [0, 1] + list(range(2, rows // TILE))[::-1]
    for block in fetch_order:
        fetch(block).start()

    def loop(low, high, step):
        def run(i, carry):
            step(i)
            return carry
        lax.fori_loop(low, high, run, 0)

    def part(i):
        return pl.ds(TILE * i, TILE)

    def wide(value):
        return jnp.concatenate([value] * (width // LANES), axis=1)

    decays = [param_ref[5, 0], param_ref[5, 1]]

    def by_bit(group, bit):
        total = jnp.float32(0.0)
        for g in range(GENES):
            total = total + jnp.where(param_ref[4, g] == float(bit), param_ref[group, g], 0.0)
        return total

    def spread(s):
        line = pl.ds(s, 1)
        bound_ref[line, :] = jnp.full((1, LANES), param_ref[6, s])
        limit_ref[line, :] = jnp.full((1, LANES), param_ref[7, s])

    def prepare():
        loop(0, count, spread)
        cols = lax.broadcasted_iota(jnp.int32, (TILE, width), 1).astype(jnp.float32)
        curve_ref[...] = width / (width + 3.0 * cols)
        fall_ref[...] = decays[1] * cols * (1.0 / width)
        first_effects = [by_bit(0, bit) for bit in range(GENES)]
        second_effects = [by_bit(1, bit) for bit in range(GENES)]
        line = lax.broadcasted_iota(jnp.int32, (TILE, LANES), 0)
        for i in range(tiles):
            state = gene * count + TILE * i + line
            one = jnp.full((TILE, LANES), 0.02, jnp.float32)
            two = jnp.full((TILE, LANES), 0.02, jnp.float32)
            for bit in range(GENES):
                held = ((state >> bit) & 1).astype(jnp.float32)
                one = one + held * first_effects[bit]
                two = two + held * second_effects[bit]
            birth_ref[part(i), :] = one
            grow_ref[part(i), :] = jnp.where(
                cols + 1.0 < wide(limit_ref[part(i), :]), wide(two), 0.0)
        for bit in range(GENES):
            rate_on = jnp.full((TILE, LANES), by_bit(2, bit))
            rate_off = jnp.full((TILE, LANES), by_bit(3, bit))
            total = rate_on + rate_off
            fading = jnp.exp(-total)
            factor_ref[bit] = (rate_off + rate_on * fading) / total
            factor_ref[GENES + bit] = rate_off * (1.0 - fading) / total
            factor_ref[2 * GENES + bit] = rate_on * (1.0 - fading) / total
            factor_ref[3 * GENES + bit] = (rate_on + rate_off * fading) / total

    def load(row):
        return x_ref[:, row, :]

    def update(buf, slot, row, out=False):
        level = (first + row).astype(jnp.float32)
        side = (total_rows + 3.0 * level) * (1.0 / (4.0 * total_rows))
        drop = decays[0] * level * (1.0 / total_rows)
        drop_next = decays[0] * (level + 1.0) * (1.0 / total_rows)
        fall, curve = fall_ref[...], curve_ref[...]
        stay = (1.0 - drop) - fall
        values = []
        for i in range(tiles):
            above = buf[slot, part(i), :]
            here = buf[slot + 1, part(i), :]
            below = buf[slot + 2, part(i), :]
            birth, bound = birth_ref[part(i), :], bound_ref[part(i), :]
            rise = wide(jnp.where(level + 1.0 < bound, birth, 0.0))
            rise_above = wide(jnp.where(level < bound, birth, 0.0))
            right = here * (grow_ref[part(i), :] * side)
            left = here * fall
            value = here * stay + drop_next * below
            value = value + curve * (rise_above * above - rise * here)
            value = value + (pltpu.roll(right, 1, 1) - right)
            values.append(value + pltpu.roll(left, width - 1, 1))
        for i, value in enumerate(values):
            if out:
                out_ref[part(i), row, :] = value
            else:
                buf[slot, part(i), :] = value

    def triangle(buf, slots, base, last):
        for t in range(1, last + 1):
            loop(0, slots - 2 * t, lambda j, t=t: update(buf, j, base + j + t))

    def wave(buf, k, out=False):
        for t in range(1, SUB + 1):
            slot = k - 2 * (t - 1)
            update(buf, slot, slot + t, out=out and t == SUB)

    def slot_of(row):
        return lax.rem(row + rows - SUB, rows)

    def mine(q, row):
        return main.at[slot_of(row)] if q == 0 else arrived[q - 1].at[row]

    forward = list(range(stages))
    backward = forward[::-1]

    def exchange(q, row, way):
        return pltpu.make_async_remote_copy(
            src_ref=mine(q, row), dst_ref=arrived[q].at[row],
            send_sem=send_sem.at[q, row], recv_sem=recv_sem.at[q, row],
            device_id=(partners[way[q]], place), device_id_type=MESH)

    def factor(kind, bit):
        return factor_ref[kind * GENES + bit]

    def mix(q, row, way):
        bit = local_bits + way[q]
        on = (gene >> way[q]) & 1 == 1
        keep = wide(jnp.where(on, factor(3, bit), factor(0, bit)))
        take = wide(jnp.where(on, factor(2, bit), factor(1, bit)))
        own = mine(q, row)
        return [keep * own[part(i), :] + take * arrived[q][row, part(i), :] for i in range(tiles)]

    def advance(q, row, way):
        exchange(q, row, way).wait_recv()
        for i, value in enumerate(mix(q, row, way)):
            arrived[q][row, part(i), :] = value
        exchange(q + 1, row, way).start()

    def finish(row, way):
        q = stages - 1
        exchange(q, row, way).wait_recv()
        blocks = mix(q, row, way)
        index = lax.broadcasted_iota(jnp.int32, (TILE, LANES), 0)
        for bit in range(3):
            on = (index >> bit) & 1 == 1
            keep = wide(jnp.where(on, factor(3, bit), factor(0, bit)))
            take = wide(jnp.where(on, factor(2, bit), factor(1, bit)))
            swap = wide(on)
            gap = 1 << bit
            mixed = []
            for block in blocks:
                other = pltpu.roll(block, gap, 0)
                if 2 * gap != TILE:
                    other = jnp.where(swap, other, pltpu.roll(block, TILE - gap, 0))
                mixed.append(keep * block + take * other)
            blocks = mixed
        for bit in range(3, local_bits):
            gap = 1 << (bit - 3)
            mixed = list(blocks)
            for i in range(tiles):
                if not i & gap:
                    low, high = blocks[i], blocks[i + gap]
                    mixed[i] = wide(factor(0, bit)) * low + wide(factor(1, bit)) * high
                    mixed[i + gap] = wide(factor(2, bit)) * low + wide(factor(3, bit)) * high
            blocks = mixed
        for i in range(tiles):
            late[row, part(i), :] = blocks[i]

    def halo(grid, rim, sends, recvs):
        upward = pltpu.make_async_remote_copy(
            src_ref=grid.at[pl.ds(rows - SUB, SUB)], dst_ref=rim.at[pl.ds(0, SUB)],
            send_sem=sends.at[0], recv_sem=recvs.at[0],
            device_id=(gene, place + 1), device_id_type=MESH)
        downward = pltpu.make_async_remote_copy(
            src_ref=rim.at[pl.ds(SUB, SUB)], dst_ref=grid.at[pl.ds(rows, SUB)],
            send_sem=sends.at[1], recv_sem=recvs.at[1],
            device_id=(gene, place - 1), device_id_type=MESH)
        return upward, downward

    def start_up(copies):
        @pl.when(has_next)
        def _():
            copies[0].start()

    def start_down(copies):
        @pl.when(has_prev)
        def _():
            copies[1].start()

    def halo_top(copies, rim):
        @pl.when(has_prev)
        def _():
            copies[1].wait_send()
            copies[0].wait_recv()

        @pl.when(jnp.logical_not(has_prev))
        def _():
            rim[pl.ds(0, SUB)] = jnp.zeros((SUB, count, width), jnp.float32)

    def halo_bottom(copies, grid):
        @pl.when(has_next)
        def _():
            copies[0].wait_send()
            copies[1].wait_recv()

        @pl.when(jnp.logical_not(has_next))
        def _():
            grid[pl.ds(rows, SUB)] = jnp.zeros((SUB, count, width), jnp.float32)

    def load_both(row):
        value = load(row)
        main[row] = value
        edge[SUB + row] = value

    def load_main(row):
        main[row] = load(row)

    prepare()
    for block in fetch_order[:2]:
        fetch(block).wait()
    loop(0, 2 * SUB, load_both)
    met = stages + jnp.where(has_prev, 1, 0) + jnp.where(has_next, 1, 0)
    pl.semaphore_wait(barrier, met)
    early_halo = halo(main, edge, halo_send, halo_recv)
    start_down(early_halo)
    triangle(main, 2 * SUB, 0, SUB - 1)

    def produce(k, way):
        @pl.when(k + 2 < rows - SUB)
        def _():
            load_main(k + 2)
        wave(main, k)
        exchange(0, k - 2, way).start()

    early = SUB + EARLY
    produce(6, backward)
    fetch(fetch_order[2]).wait()
    loop(rows - SUB, rows, load_main)
    start_up(early_halo)
    for block in fetch_order[3:]:
        fetch(block).wait()
    loop(7, early + 2, lambda k: produce(k, backward))
    loop(early + 2, rows - SUB, lambda k: produce(k, forward))
    halo_bottom(early_halo, main)
    loop(rows - SUB, rows + 2, lambda k: produce(k, forward))
    halo_top(early_halo, edge)
    triangle(edge, 3 * SUB, -SUB, SUB)

    def give(row):
        main[rows - SUB + row] = edge[row]
        exchange(0, row, forward).start()

    loop(0, SUB, give)
    order = [
        (rows - SUB, rows, forward), (0, SUB, forward), (early, rows - SUB, forward),
        (SUB, early, backward),
    ]
    for q in range(stages - 1):
        for low, high, way in order:
            loop(low, high, lambda row, q=q, way=way: advance(q, row, way))

    for low, high, way in order[3:] + order[:2]:
        loop(low, high, lambda row, way=way: finish(row, way))

    def copy_edge(row):
        late_edge[SUB + row] = late[row]

    loop(0, 2 * SUB, copy_edge)
    late_halo = halo(late, late_edge, late_send, late_recv)
    start_down(late_halo)
    start_up(late_halo)

    def emit(k):
        wave(late, k, out=True)

    def finish_and_emit(k):
        finish(k + 2, forward)
        emit(k)

    triangle(late, 2 * SUB, 0, SUB - 1)
    loop(6, early - 2, emit)
    loop(early - 2, rows - SUB - 6, finish_and_emit)
    halo_top(late_halo, late_edge)
    triangle(late_edge, 3 * SUB, -SUB, SUB - 1)
    loop(0, SUB, lambda j: update(late_edge, j, j, out=True))
    loop(rows - SUB - 6, rows - SUB - 2, finish_and_emit)
    halo_bottom(late_halo, late)
    loop(rows - SUB - 2, rows + 2, emit)
    for q in range(stages):
        for low, high, way in order:
            loop(low, high, lambda row, q=q, way=way: exchange(q, row, way).wait_send())


def body(
    peers, genes, density, effect_first, effect_second, decay_pair, switch_rates, gene_place,
    bound_first, bound_second,
):
    count, rows, width = density.shape
    pieces = [
        effect_first[None], effect_second[None], switch_rates, gene_place[None], decay_pair[None],
        bound_first[None], bound_second[None]]
    sums = {np.float32: 0.0, np.int32: 0}
    line = 0
    for piece in pieces:
        after = TILE - line - piece.shape[0]
        kind = piece.dtype.type
        sums[kind] += jnp.pad(piece, ((line, after), (0, LANES - piece.shape[1])))
        line += piece.shape[0]
    params = sums[np.float32] + sums[np.int32].astype(jnp.float32)
    stages = genes.bit_length() - 1
    row = (count, width)

    def vmem(*shape):
        return pltpu.VMEM(shape, jnp.float32)

    return pl.pallas_call(
        functools.partial(kernel, count, rows, width, peers, float(rows * peers)),
        out_shape=jax.ShapeDtypeStruct(density.shape, jnp.float32),
        in_specs=[
            pl.BlockSpec(memory_space=pl.ANY), pl.BlockSpec(memory_space=pltpu.SMEM)],
        out_specs=pl.BlockSpec(memory_space=pltpu.VMEM),
        scratch_shapes=[
            vmem(*density.shape),
            vmem(count, LANES),
            vmem(count, LANES),
            vmem(count, LANES),
            vmem(*row),
            vmem(TILE, width),
            vmem(TILE, width),
            vmem(4 * GENES, TILE, LANES),
            vmem(rows + SUB, *row),
            vmem(3 * SUB, *row),
            vmem(rows + SUB, *row),
            vmem(3 * SUB, *row),
        ] + [vmem(rows, *row)] * stages + [
            pltpu.SemaphoreType.DMA((stages, rows)),
            pltpu.SemaphoreType.DMA((stages, rows)),
            pltpu.SemaphoreType.DMA((2,)),
            pltpu.SemaphoreType.DMA((2,)),
            pltpu.SemaphoreType.DMA((2,)),
            pltpu.SemaphoreType.DMA((2,)),
            pltpu.SemaphoreType.DMA((rows // TILE,)),
        ],
        compiler_params=pltpu.CompilerParams(
            collective_id=0, has_side_effects=True, vmem_limit_bytes=48 * 1024 * 1024),
    )(density, params)


def solution(mesh):
    placed = (P("gene", "rows", None), P(), P(), P(), P(), P(), P("gene"), P("gene"))
    return jax.shard_map(
        functools.partial(body, mesh.shape["rows"], mesh.shape["gene"]),
        mesh=mesh, in_specs=placed, out_specs=P("gene", "rows", None), check_vma=False,
    )
```

```python
import functools

import jax
import jax.numpy as jnp
import numpy as np
from jax import lax
from jax.experimental import pallas as pl
from jax.experimental.pallas import tpu as pltpu
from jax.sharding import PartitionSpec as P

GENES = 7
SUB = 4
TILE = 8
LANES = 128
EARLY = 11
MESH = pl.DeviceIdType.MESH


def kernel(
    count, rows, width, peers, total_rows,
    density_ref, param_ref, out_ref,
    x_ref, birth_ref, bound_ref, limit_ref, grow_ref, curve_ref, fall_ref, factor_ref,
    main, edge, late, late_edge, foot, *rest,
):
    stages = len(rest) - 7
    arrived = rest[:stages]
    send_sem, recv_sem, halo_send, halo_recv, late_send, late_recv, in_sem = rest[stages:]
    tiles = count // TILE
    local_bits = count.bit_length() - 1
    gene = lax.axis_index("gene")
    place = lax.axis_index("rows")
    first = place * rows
    partners = [gene + (1 << q) - 2 * (gene & (1 << q)) for q in range(stages)]
    has_prev, has_next = place > 0, place < peers - 1

    barrier = pltpu.get_barrier_semaphore()
    for partner in partners:
        pl.semaphore_signal(barrier, inc=1, device_id=(partner, place), device_id_type=MESH)

    @pl.when(has_prev)
    def _():
        pl.semaphore_signal(barrier, inc=1, device_id=(gene, place - 1), device_id_type=MESH)

    @pl.when(has_next)
    def _():
        pl.semaphore_signal(barrier, inc=1, device_id=(gene, place + 1), device_id_type=MESH)

    def fetch(block):
        piece = pl.ds(TILE * block, TILE)
        return pltpu.make_async_copy(
            density_ref.at[:, piece, :], x_ref.at[:, piece, :], in_sem.at[block])

    fetch_order = [0, 1] + list(range(2, rows // TILE))[::-1]
    for block in fetch_order:
        fetch(block).start()

    def loop(low, high, step):
        def run(i, carry):
            step(i)
            return carry
        lax.fori_loop(low, high, run, 0)

    def part(i):
        return pl.ds(TILE * i, TILE)

    def wide(value):
        return jnp.concatenate([value] * (width // LANES), axis=1)

    decays = [param_ref[5, 0], param_ref[5, 1]]

    def by_bit(group, bit):
        total = jnp.float32(0.0)
        for g in range(GENES):
            total = total + jnp.where(param_ref[4, g] == float(bit), param_ref[group, g], 0.0)
        return total

    def spread(s):
        line = pl.ds(s, 1)
        bound_ref[line, :] = jnp.full((1, LANES), param_ref[6, s])
        limit_ref[line, :] = jnp.full((1, LANES), param_ref[7, s])

    def prepare():
        loop(0, count, spread)
        cols = lax.broadcasted_iota(jnp.int32, (TILE, width), 1).astype(jnp.float32)
        curve_ref[...] = width / (width + 3.0 * cols)
        fall_ref[...] = decays[1] * cols * (1.0 / width)
        first_effects = [by_bit(0, bit) for bit in range(GENES)]
        second_effects = [by_bit(1, bit) for bit in range(GENES)]
        line = lax.broadcasted_iota(jnp.int32, (TILE, LANES), 0)
        for i in range(tiles):
            state = gene * count + TILE * i + line
            one = jnp.full((TILE, LANES), 0.02, jnp.float32)
            two = jnp.full((TILE, LANES), 0.02, jnp.float32)
            for bit in range(GENES):
                held = ((state >> bit) & 1).astype(jnp.float32)
                one = one + held * first_effects[bit]
                two = two + held * second_effects[bit]
            birth_ref[part(i), :] = one
            grow_ref[part(i), :] = jnp.where(
                cols + 1.0 < wide(limit_ref[part(i), :]), wide(two), 0.0)

    def prepare_factors():
        for bit in range(GENES):
            rate_on = jnp.full((TILE, LANES), by_bit(2, bit))
            rate_off = jnp.full((TILE, LANES), by_bit(3, bit))
            total = rate_on + rate_off
            fading = jnp.exp(-total)
            factor_ref[bit] = (rate_off + rate_on * fading) / total
            factor_ref[GENES + bit] = rate_off * (1.0 - fading) / total
            factor_ref[2 * GENES + bit] = rate_on * (1.0 - fading) / total
            factor_ref[3 * GENES + bit] = (rate_on + rate_off * fading) / total

    def load(row):
        return x_ref[:, row, :]

    def update(buf, slot, row, out=False, to=None):
        level = (first + row).astype(jnp.float32)
        side = (total_rows + 3.0 * level) * (1.0 / (4.0 * total_rows))
        drop = decays[0] * level * (1.0 / total_rows)
        drop_next = decays[0] * (level + 1.0) * (1.0 / total_rows)
        fall, curve = fall_ref[...], curve_ref[...]
        stay = (1.0 - drop) - fall
        values = []
        for i in range(tiles):
            above = buf[slot, part(i), :]
            here = buf[slot + 1, part(i), :]
            below = buf[slot + 2, part(i), :]
            birth, bound = birth_ref[part(i), :], bound_ref[part(i), :]
            rise = wide(jnp.where(level + 1.0 < bound, birth, 0.0))
            rise_above = wide(jnp.where(level < bound, birth, 0.0))
            right = here * (grow_ref[part(i), :] * side)
            left = here * fall
            value = here * stay + drop_next * below
            value = value + curve * (rise_above * above - rise * here)
            value = value + (pltpu.roll(right, 1, 1) - right)
            values.append(value + pltpu.roll(left, width - 1, 1))
        for i, value in enumerate(values):
            if out:
                out_ref[part(i), row, :] = value
            elif to is not None:
                foot[to, part(i), :] = value
            else:
                buf[slot, part(i), :] = value

    def triangle(buf, slots, base, last):
        for t in range(1, last + 1):
            loop(0, slots - 2 * t, lambda j, t=t: update(buf, j, base + j + t))

    def wave(buf, k, out=False):
        for t in range(1, SUB + 1):
            slot = k - 2 * (t - 1)
            update(buf, slot, slot + t, out=out and t == SUB)

    def slot_of(row):
        return lax.rem(row + rows - SUB, rows)

    def mine(q, row):
        return main.at[slot_of(row)] if q == 0 else arrived[q - 1].at[row]

    forward = list(range(stages))
    backward = forward[::-1]

    def exchange(q, row, way):
        return pltpu.make_async_remote_copy(
            src_ref=mine(q, row), dst_ref=arrived[q].at[row],
            send_sem=send_sem.at[q, row], recv_sem=recv_sem.at[q, row],
            device_id=(partners[way[q]], place), device_id_type=MESH)

    def factor(kind, bit):
        return factor_ref[kind * GENES + bit]

    def mix(q, row, way):
        bit = local_bits + way[q]
        on = (gene >> way[q]) & 1 == 1
        keep = wide(jnp.where(on, factor(3, bit), factor(0, bit)))
        take = wide(jnp.where(on, factor(2, bit), factor(1, bit)))
        own = mine(q, row)
        return [keep * own[part(i), :] + take * arrived[q][row, part(i), :] for i in range(tiles)]

    def advance(q, row, way):
        exchange(q, row, way).wait_recv()
        for i, value in enumerate(mix(q, row, way)):
            arrived[q][row, part(i), :] = value
        exchange(q + 1, row, way).start()

    def finish(row, way):
        q = stages - 1
        exchange(q, row, way).wait_recv()
        blocks = mix(q, row, way)
        index = lax.broadcasted_iota(jnp.int32, (TILE, LANES), 0)
        for bit in range(3):
            on = (index >> bit) & 1 == 1
            keep = wide(jnp.where(on, factor(3, bit), factor(0, bit)))
            take = wide(jnp.where(on, factor(2, bit), factor(1, bit)))
            swap = wide(on)
            gap = 1 << bit
            mixed = []
            for block in blocks:
                other = pltpu.roll(block, gap, 0)
                if 2 * gap != TILE:
                    other = jnp.where(swap, other, pltpu.roll(block, TILE - gap, 0))
                mixed.append(keep * block + take * other)
            blocks = mixed
        for bit in range(3, local_bits):
            gap = 1 << (bit - 3)
            mixed = list(blocks)
            for i in range(tiles):
                if not i & gap:
                    low, high = blocks[i], blocks[i + gap]
                    mixed[i] = wide(factor(0, bit)) * low + wide(factor(1, bit)) * high
                    mixed[i + gap] = wide(factor(2, bit)) * low + wide(factor(3, bit)) * high
            blocks = mixed
        for i in range(tiles):
            late[row, part(i), :] = blocks[i]

    def halo(grid, rim, sends, recvs):
        upward = pltpu.make_async_remote_copy(
            src_ref=grid.at[pl.ds(rows - SUB, SUB)], dst_ref=rim.at[pl.ds(0, SUB)],
            send_sem=sends.at[0], recv_sem=recvs.at[0],
            device_id=(gene, place + 1), device_id_type=MESH)
        downward = pltpu.make_async_remote_copy(
            src_ref=rim.at[pl.ds(SUB, SUB)], dst_ref=grid.at[pl.ds(rows, SUB)],
            send_sem=sends.at[1], recv_sem=recvs.at[1],
            device_id=(gene, place - 1), device_id_type=MESH)
        return upward, downward

    def start_up(copies):
        @pl.when(has_next)
        def _():
            copies[0].start()

    def start_down(copies):
        @pl.when(has_prev)
        def _():
            copies[1].start()

    def halo_top(copies, rim):
        @pl.when(has_prev)
        def _():
            copies[1].wait_send()
            copies[0].wait_recv()

        @pl.when(jnp.logical_not(has_prev))
        def _():
            rim[pl.ds(0, SUB)] = jnp.zeros((SUB, count, width), jnp.float32)

    def halo_bottom(copies, grid):
        @pl.when(has_next)
        def _():
            copies[0].wait_send()
            copies[1].wait_recv()

        @pl.when(jnp.logical_not(has_next))
        def _():
            grid[pl.ds(rows, SUB)] = jnp.zeros((SUB, count, width), jnp.float32)

    def load_both(row):
        value = load(row)
        main[row] = value
        edge[SUB + row] = value

    def load_main(row):
        main[row] = load(row)

    prepare()
    for block in fetch_order[:2]:
        fetch(block).wait()
    loop(0, 2 * SUB, load_both)
    met = stages + jnp.where(has_prev, 1, 0) + jnp.where(has_next, 1, 0)
    pl.semaphore_wait(barrier, met)
    early_halo = halo(main, edge, halo_send, halo_recv)
    start_down(early_halo)
    triangle(main, 2 * SUB, 0, SUB - 1)

    def produce(k, way):
        @pl.when(k + 2 < rows - SUB)
        def _():
            load_main(k + 2)
        wave(main, k)
        exchange(0, k - 2, way).start()

    early = SUB + EARLY
    produce(6, backward)
    prepare_factors()
    fetch(fetch_order[2]).wait()
    loop(rows - SUB, rows, load_main)
    start_up(early_halo)
    for block in fetch_order[3:]:
        fetch(block).wait()
    loop(7, early + 2, lambda k: produce(k, backward))
    loop(early + 2, rows - SUB, lambda k: produce(k, forward))
    halo_bottom(early_halo, main)
    loop(rows - SUB, rows + 2, lambda k: produce(k, forward))
    loop(rows - SUB, rows, lambda row: advance(0, row, forward))
    halo_top(early_halo, edge)
    triangle(edge, 3 * SUB, -SUB, SUB)

    def give(row):
        main[rows - SUB + row] = edge[row]
        exchange(0, row, forward).start()

    loop(0, SUB, give)
    order = [
        (rows - SUB, rows, forward), (0, SUB, forward), (early, rows - SUB, forward),
        (SUB, early, backward),
    ]
    for q in range(stages - 1):
        for low, high, way in order[1 if q == 0 else 0:]:
            loop(low, high, lambda row, q=q, way=way: advance(q, row, way))

    for low, high, way in order[3:] + order[:2]:
        loop(low, high, lambda row, way=way: finish(row, way))

    def copy_edge(row):
        late_edge[SUB + row] = late[row]

    loop(0, 2 * SUB, copy_edge)
    late_halo = halo(late, late_edge, late_send, late_recv)
    start_down(late_halo)
    start_up(late_halo)

    def emit(k):
        wave(late, k, out=True)

    def finish_and_emit(k):
        finish(k + 2, forward)
        emit(k)

    triangle(late, 2 * SUB, 0, SUB - 1)
    loop(6, early - 2, emit)
    loop(early - 2, rows - SUB - 6, finish_and_emit)
    halo_top(late_halo, late_edge)
    triangle(late_edge, 3 * SUB, -SUB, SUB - 1)
    loop(0, SUB, lambda j: update(late_edge, j, j, out=True))
    last = rows - SUB - 1
    loop(rows - SUB - 6, last - 2, finish_and_emit)
    halo_bottom(late_halo, late)
    starts = [0, 6, 10, 12]
    loop(0, 6, lambda j: update(late, last + 1 + j, last + 2 + j, to=j))
    for t in range(2, SUB):
        begin, end = starts[t - 1], starts[t]
        before = starts[t - 2]
        loop(0, end - begin, lambda j, t=t, begin=begin, before=before: update(
            foot, before + j, last + 1 + t + j, to=begin + j))
    finish(last, forward)
    for t in range(1, SUB + 1):
        loop(last - t, last + t + 1, lambda row, t=t: update(late, row - t, row, out=t == SUB))
        if t < SUB:
            for i in range(2):
                late[last + 1 + i] = foot[starts[t - 1] + i]
    for q in range(stages):
        for low, high, way in order:
            loop(low, high, lambda row, q=q, way=way: exchange(q, row, way).wait_send())


def body(
    peers, genes, density, effect_first, effect_second, decay_pair, switch_rates, gene_place,
    bound_first, bound_second,
):
    count, rows, width = density.shape
    pieces = [
        effect_first[None], effect_second[None], switch_rates, gene_place[None], decay_pair[None],
        bound_first[None], bound_second[None]]
    sums = {np.float32: 0.0, np.int32: 0}
    line = 0
    for piece in pieces:
        after = TILE - line - piece.shape[0]
        kind = piece.dtype.type
        sums[kind] += jnp.pad(piece, ((line, after), (0, LANES - piece.shape[1])))
        line += piece.shape[0]
    params = sums[np.float32] + sums[np.int32].astype(jnp.float32)
    stages = genes.bit_length() - 1
    row = (count, width)

    def vmem(*shape):
        return pltpu.VMEM(shape, jnp.float32)

    return pl.pallas_call(
        functools.partial(kernel, count, rows, width, peers, float(rows * peers)),
        out_shape=jax.ShapeDtypeStruct(density.shape, jnp.float32),
        in_specs=[
            pl.BlockSpec(memory_space=pl.ANY), pl.BlockSpec(memory_space=pltpu.SMEM)],
        out_specs=pl.BlockSpec(memory_space=pltpu.VMEM),
        scratch_shapes=[
            vmem(*density.shape),
            vmem(count, LANES),
            vmem(count, LANES),
            vmem(count, LANES),
            vmem(*row),
            vmem(TILE, width),
            vmem(TILE, width),
            vmem(4 * GENES, TILE, LANES),
            vmem(rows + SUB, *row),
            vmem(3 * SUB, *row),
            vmem(rows + SUB, *row),
            vmem(3 * SUB, *row),
            vmem(3 * SUB, *row),
        ] + [vmem(rows, *row)] * stages + [
            pltpu.SemaphoreType.DMA((stages, rows)),
            pltpu.SemaphoreType.DMA((stages, rows)),
            pltpu.SemaphoreType.DMA((2,)),
            pltpu.SemaphoreType.DMA((2,)),
            pltpu.SemaphoreType.DMA((2,)),
            pltpu.SemaphoreType.DMA((2,)),
            pltpu.SemaphoreType.DMA((rows // TILE,)),
        ],
        compiler_params=pltpu.CompilerParams(
            collective_id=0, has_side_effects=True, vmem_limit_bytes=48 * 1024 * 1024),
    )(density, params)


def solution(mesh):
    placed = (P("gene", "rows", None), P(), P(), P(), P(), P(), P("gene"), P("gene"))
    return jax.shard_map(
        functools.partial(body, mesh.shape["rows"], mesh.shape["gene"]),
        mesh=mesh, in_specs=placed, out_specs=P("gene", "rows", None), check_vma=False,
    )
```

```python
import functools

import jax
import jax.numpy as jnp
import numpy as np
from jax import lax
from jax.experimental import pallas as pl
from jax.experimental.pallas import tpu as pltpu
from jax.sharding import PartitionSpec as P

GENES = 7
SUB = 4
TILE = 8
LANES = 128
EARLY = 11
MESH = pl.DeviceIdType.MESH


def kernel(
    count, rows, width, peers, total_rows,
    density_ref, param_ref, out_ref,
    x_ref, birth_ref, bound_ref, limit_ref, grow_ref, curve_ref, fall_ref, factor_ref,
    main, edge, late, late_edge, foot, *rest,
):
    stages = len(rest) - 7
    arrived = rest[:stages]
    send_sem, recv_sem, halo_send, halo_recv, late_send, late_recv, in_sem = rest[stages:]
    tiles = count // TILE
    local_bits = count.bit_length() - 1
    gene = lax.axis_index("gene")
    place = lax.axis_index("rows")
    first = place * rows
    partners = [gene + (1 << q) - 2 * (gene & (1 << q)) for q in range(stages)]
    has_prev, has_next = place > 0, place < peers - 1

    barrier = pltpu.get_barrier_semaphore()
    for partner in partners:
        pl.semaphore_signal(barrier, inc=1, device_id=(partner, place), device_id_type=MESH)

    @pl.when(has_prev)
    def _():
        pl.semaphore_signal(barrier, inc=1, device_id=(gene, place - 1), device_id_type=MESH)

    @pl.when(has_next)
    def _():
        pl.semaphore_signal(barrier, inc=1, device_id=(gene, place + 1), device_id_type=MESH)

    def fetch(block):
        piece = pl.ds(TILE * block, TILE)
        return pltpu.make_async_copy(
            density_ref.at[:, piece, :], x_ref.at[:, piece, :], in_sem.at[block])

    fetch_order = [0, 1] + list(range(2, rows // TILE))[::-1]
    for block in fetch_order:
        fetch(block).start()

    def loop(low, high, step):
        def run(i, carry):
            step(i)
            return carry
        lax.fori_loop(low, high, run, 0)

    def part(i):
        return pl.ds(TILE * i, TILE)

    def wide(value):
        return jnp.concatenate([value] * (width // LANES), axis=1)

    decays = [param_ref[5, 0], param_ref[5, 1]]

    def by_bit(group, bit):
        total = jnp.float32(0.0)
        for g in range(GENES):
            total = total + jnp.where(param_ref[4, g] == float(bit), param_ref[group, g], 0.0)
        return total

    def spread(s):
        line = pl.ds(s, 1)
        bound_ref[line, :] = jnp.full((1, LANES), param_ref[6, s])
        limit_ref[line, :] = jnp.full((1, LANES), param_ref[7, s])

    def prepare():
        loop(0, count, spread)
        cols = lax.broadcasted_iota(jnp.int32, (TILE, width), 1).astype(jnp.float32)
        curve_ref[...] = width / (width + 3.0 * cols)
        fall_ref[...] = decays[1] * cols * (1.0 / width)
        first_effects = [by_bit(0, bit) for bit in range(GENES)]
        second_effects = [by_bit(1, bit) for bit in range(GENES)]
        line = lax.broadcasted_iota(jnp.int32, (TILE, LANES), 0)
        for i in range(tiles):
            state = gene * count + TILE * i + line
            one = jnp.full((TILE, LANES), 0.02, jnp.float32)
            two = jnp.full((TILE, LANES), 0.02, jnp.float32)
            for bit in range(GENES):
                held = ((state >> bit) & 1).astype(jnp.float32)
                one = one + held * first_effects[bit]
                two = two + held * second_effects[bit]
            birth_ref[part(i), :] = one
            grow_ref[part(i), :] = jnp.where(
                cols + 1.0 < wide(limit_ref[part(i), :]), wide(two), 0.0)

    def prepare_factors():
        for bit in range(GENES):
            rate_on = jnp.full((TILE, LANES), by_bit(2, bit))
            rate_off = jnp.full((TILE, LANES), by_bit(3, bit))
            total = rate_on + rate_off
            fading = jnp.exp(-total)
            factor_ref[bit] = (rate_off + rate_on * fading) / total
            factor_ref[GENES + bit] = rate_off * (1.0 - fading) / total
            factor_ref[2 * GENES + bit] = rate_on * (1.0 - fading) / total
            factor_ref[3 * GENES + bit] = (rate_on + rate_off * fading) / total

    def load(row):
        return x_ref[:, row, :]

    def update(buf, slot, row, out=False, to=None):
        level = (first + row).astype(jnp.float32)
        side = (total_rows + 3.0 * level) * (1.0 / (4.0 * total_rows))
        drop = decays[0] * level * (1.0 / total_rows)
        drop_next = decays[0] * (level + 1.0) * (1.0 / total_rows)
        fall, curve = fall_ref[...], curve_ref[...]
        stay = (1.0 - drop) - fall
        values = []
        for i in range(tiles):
            above = buf[slot, part(i), :]
            here = buf[slot + 1, part(i), :]
            below = buf[slot + 2, part(i), :]
            birth, bound = birth_ref[part(i), :], bound_ref[part(i), :]
            rise = wide(jnp.where(level + 1.0 < bound, birth, 0.0))
            rise_above = wide(jnp.where(level < bound, birth, 0.0))
            right = here * (grow_ref[part(i), :] * side)
            left = here * fall
            value = here * stay + drop_next * below
            value = value + curve * (rise_above * above - rise * here)
            value = value + (pltpu.roll(right, 1, 1) - right)
            values.append(value + pltpu.roll(left, width - 1, 1))
        for i, value in enumerate(values):
            if out:
                out_ref[part(i), row, :] = value
            elif to is not None:
                foot[to, part(i), :] = value
            else:
                buf[slot, part(i), :] = value

    def triangle(buf, slots, base, last):
        for t in range(1, last + 1):
            loop(0, slots - 2 * t, lambda j, t=t: update(buf, j, base + j + t))

    def wave(buf, k, out=False):
        for t in range(1, SUB + 1):
            slot = k - 2 * (t - 1)
            update(buf, slot, slot + t, out=out and t == SUB)

    def slot_of(row):
        return lax.rem(row + rows - SUB, rows)

    def mine(q, row):
        return main.at[slot_of(row)] if q == 0 else arrived[q - 1].at[row]

    forward = list(range(stages))
    backward = forward[::-1]

    def exchange(q, row, way):
        return pltpu.make_async_remote_copy(
            src_ref=mine(q, row), dst_ref=arrived[q].at[row],
            send_sem=send_sem.at[q, row], recv_sem=recv_sem.at[q, row],
            device_id=(partners[way[q]], place), device_id_type=MESH)

    def factor(kind, bit):
        return factor_ref[kind * GENES + bit]

    def mix(q, row, way):
        bit = local_bits + way[q]
        on = (gene >> way[q]) & 1 == 1
        keep = wide(jnp.where(on, factor(3, bit), factor(0, bit)))
        take = wide(jnp.where(on, factor(2, bit), factor(1, bit)))
        own = mine(q, row)
        return [keep * own[part(i), :] + take * arrived[q][row, part(i), :] for i in range(tiles)]

    def advance(q, row, way):
        exchange(q, row, way).wait_recv()
        for i, value in enumerate(mix(q, row, way)):
            arrived[q][row, part(i), :] = value
        exchange(q + 1, row, way).start()

    def finish(row, way):
        q = stages - 1
        exchange(q, row, way).wait_recv()
        blocks = mix(q, row, way)
        index = lax.broadcasted_iota(jnp.int32, (TILE, LANES), 0)
        for bit in range(3):
            on = (index >> bit) & 1 == 1
            keep = wide(jnp.where(on, factor(3, bit), factor(0, bit)))
            take = wide(jnp.where(on, factor(2, bit), factor(1, bit)))
            swap = wide(on)
            gap = 1 << bit
            mixed = []
            for block in blocks:
                other = pltpu.roll(block, gap, 0)
                if 2 * gap != TILE:
                    other = jnp.where(swap, other, pltpu.roll(block, TILE - gap, 0))
                mixed.append(keep * block + take * other)
            blocks = mixed
        for bit in range(3, local_bits):
            gap = 1 << (bit - 3)
            mixed = list(blocks)
            for i in range(tiles):
                if not i & gap:
                    low, high = blocks[i], blocks[i + gap]
                    mixed[i] = wide(factor(0, bit)) * low + wide(factor(1, bit)) * high
                    mixed[i + gap] = wide(factor(2, bit)) * low + wide(factor(3, bit)) * high
            blocks = mixed
        for i in range(tiles):
            late[row, part(i), :] = blocks[i]

    def halo(grid, rim, sends, recvs):
        upward = pltpu.make_async_remote_copy(
            src_ref=grid.at[pl.ds(rows - SUB, SUB)], dst_ref=rim.at[pl.ds(0, SUB)],
            send_sem=sends.at[0], recv_sem=recvs.at[0],
            device_id=(gene, place + 1), device_id_type=MESH)
        downward = pltpu.make_async_remote_copy(
            src_ref=rim.at[pl.ds(SUB, SUB)], dst_ref=grid.at[pl.ds(rows, SUB)],
            send_sem=sends.at[1], recv_sem=recvs.at[1],
            device_id=(gene, place - 1), device_id_type=MESH)
        return upward, downward

    def start_up(copies):
        @pl.when(has_next)
        def _():
            copies[0].start()

    def start_down(copies):
        @pl.when(has_prev)
        def _():
            copies[1].start()

    def halo_top(copies, rim):
        @pl.when(has_prev)
        def _():
            copies[1].wait_send()
            copies[0].wait_recv()

        @pl.when(jnp.logical_not(has_prev))
        def _():
            rim[pl.ds(0, SUB)] = jnp.zeros((SUB, count, width), jnp.float32)

    def halo_bottom(copies, grid):
        @pl.when(has_next)
        def _():
            copies[0].wait_send()
            copies[1].wait_recv()

        @pl.when(jnp.logical_not(has_next))
        def _():
            grid[pl.ds(rows, SUB)] = jnp.zeros((SUB, count, width), jnp.float32)

    def load_both(row):
        value = load(row)
        main[row] = value
        edge[SUB + row] = value

    def load_main(row):
        main[row] = load(row)

    prepare()
    for block in fetch_order[:2]:
        fetch(block).wait()
    loop(0, 2 * SUB, load_both)
    met = stages + jnp.where(has_prev, 1, 0) + jnp.where(has_next, 1, 0)
    pl.semaphore_wait(barrier, met)
    early_halo = halo(main, edge, halo_send, halo_recv)
    start_down(early_halo)
    triangle(main, 2 * SUB, 0, SUB - 1)

    def produce(k, way):
        @pl.when(k + 2 < rows - SUB)
        def _():
            load_main(k + 2)
        wave(main, k)
        exchange(0, k - 2, way).start()

    early = SUB + EARLY
    produce(6, backward)
    prepare_factors()
    fetch(fetch_order[2]).wait()
    loop(rows - SUB, rows, load_main)
    start_up(early_halo)
    for block in fetch_order[3:]:
        fetch(block).wait()
    loop(7, early + 2, lambda k: produce(k, backward))
    loop(early + 2, rows - SUB, lambda k: produce(k, forward))
    halo_bottom(early_halo, main)
    loop(rows - SUB, rows + 2, lambda k: produce(k, forward))
    loop(rows - SUB, rows, lambda row: advance(0, row, forward))
    halo_top(early_halo, edge)
    triangle(edge, 3 * SUB, -SUB, SUB)

    def give(row):
        main[rows - SUB + row] = edge[row]
        exchange(0, row, forward).start()

    loop(0, SUB, give)
    order = [
        (rows - SUB, rows, forward), (0, SUB, forward), (early, rows - SUB, forward),
        (SUB, early, backward),
    ]
    for q in range(stages - 1):
        for low, high, way in order[1 if q == 0 else 0:]:
            loop(low, high, lambda row, q=q, way=way: advance(q, row, way))

    for low, high, way in order[3:] + order[:2]:
        loop(low, high, lambda row, way=way: finish(row, way))

    def copy_edge(row):
        late_edge[SUB + row] = late[row]

    loop(0, 2 * SUB, copy_edge)
    late_halo = halo(late, late_edge, late_send, late_recv)
    start_down(late_halo)
    start_up(late_halo)

    def emit(k):
        wave(late, k, out=True)

    def finish_and_emit(k):
        finish(k + 2, forward)
        emit(k)

    triangle(late, 2 * SUB, 0, SUB - 1)
    loop(6, early - 2, emit)
    loop(early - 2, rows - SUB - 6, finish_and_emit)
    halo_top(late_halo, late_edge)
    triangle(late_edge, 3 * SUB, -SUB, SUB - 1)
    loop(0, SUB, lambda j: update(late_edge, j, j, out=True))
    last = rows - SUB - 1
    loop(rows - SUB - 6, last - 2, finish_and_emit)
    halo_bottom(late_halo, late)
    starts = [0, 6, 10, 12]
    loop(0, 6, lambda j: update(late, last + 1 + j, last + 2 + j, to=j))
    for t in range(2, SUB):
        begin, end = starts[t - 1], starts[t]
        before = starts[t - 2]
        loop(0, end - begin, lambda j, t=t, begin=begin, before=before: update(
            foot, before + j, last + 1 + t + j, to=begin + j))
    for q in range(stages):
        for low, high, way in order:
            high = high - SUB if high == last + 1 else high
            loop(low, high, lambda row, q=q, way=way: exchange(q, row, way).wait_send())
    finish(last, forward)
    for t in range(1, SUB + 1):
        loop(last - t, last + t + 1, lambda row, t=t: update(late, row - t, row, out=t == SUB))
        if t < SUB:
            for i in range(2):
                late[last + 1 + i] = foot[starts[t - 1] + i]
    for q in range(stages):
        loop(last - SUB + 1, last + 1, lambda row, q=q: exchange(q, row, forward).wait_send())


def body(
    peers, genes, density, effect_first, effect_second, decay_pair, switch_rates, gene_place,
    bound_first, bound_second,
):
    count, rows, width = density.shape
    pieces = [
        effect_first[None], effect_second[None], switch_rates, gene_place[None], decay_pair[None],
        bound_first[None], bound_second[None]]
    sums = {np.float32: 0.0, np.int32: 0}
    line = 0
    for piece in pieces:
        after = TILE - line - piece.shape[0]
        kind = piece.dtype.type
        sums[kind] += jnp.pad(piece, ((line, after), (0, LANES - piece.shape[1])))
        line += piece.shape[0]
    params = sums[np.float32] + sums[np.int32].astype(jnp.float32)
    stages = genes.bit_length() - 1
    row = (count, width)

    def vmem(*shape):
        return pltpu.VMEM(shape, jnp.float32)

    return pl.pallas_call(
        functools.partial(kernel, count, rows, width, peers, float(rows * peers)),
        out_shape=jax.ShapeDtypeStruct(density.shape, jnp.float32),
        in_specs=[
            pl.BlockSpec(memory_space=pl.ANY), pl.BlockSpec(memory_space=pltpu.SMEM)],
        out_specs=pl.BlockSpec(memory_space=pltpu.VMEM),
        scratch_shapes=[
            vmem(*density.shape),
            vmem(count, LANES),
            vmem(count, LANES),
            vmem(count, LANES),
            vmem(*row),
            vmem(TILE, width),
            vmem(TILE, width),
            vmem(4 * GENES, TILE, LANES),
            vmem(rows + SUB, *row),
            vmem(3 * SUB, *row),
            vmem(rows + SUB, *row),
            vmem(3 * SUB, *row),
            vmem(3 * SUB, *row),
        ] + [vmem(rows, *row)] * stages + [
            pltpu.SemaphoreType.DMA((stages, rows)),
            pltpu.SemaphoreType.DMA((stages, rows)),
            pltpu.SemaphoreType.DMA((2,)),
            pltpu.SemaphoreType.DMA((2,)),
            pltpu.SemaphoreType.DMA((2,)),
            pltpu.SemaphoreType.DMA((2,)),
            pltpu.SemaphoreType.DMA((rows // TILE,)),
        ],
        compiler_params=pltpu.CompilerParams(
            collective_id=0, has_side_effects=True, vmem_limit_bytes=48 * 1024 * 1024),
    )(density, params)


def solution(mesh):
    placed = (P("gene", "rows", None), P(), P(), P(), P(), P(), P("gene"), P("gene"))
    return jax.shard_map(
        functools.partial(body, mesh.shape["rows"], mesh.shape["gene"]),
        mesh=mesh, in_specs=placed, out_specs=P("gene", "rows", None), check_vma=False,
    )
```
